32 devices in a mesh: group: 2 (over x), seq: 16 (over z, y, core).
Axes of the slice: x: 2, y: 2, z: 4, core: 2. Of those that a mesh axis runs over, the one named last changes fastest.
Arguments:
- queries: bfloat16 [4096, 4096], P(('group', 'seq')), parts along dimension 0, may hold values from -20 to 20
- response_keys: bfloat16 [4096, 512], P(('group', 'seq')), parts along dimension 0, may hold values from -6 to 6
- response_values: bfloat16 [4096, 512], P(('group', 'seq')), parts along dimension 0, may hold values from -6 to 6
- output_grad: bfloat16 [4096, 4096], P(('group', 'seq')), parts along dimension 0, may hold values from -6 to 6
- prompt_keys: bfloat16 [2048, 512], P(('group', 'seq')), parts along dimension 0, may hold values from -6 to 6
- prompt_values: bfloat16 [2048, 512], P(('group', 'seq')), parts along dimension 0, may hold values from -6 to 6
- block_list: int32 [32, 12], P('group'), parts along dimension 0, may hold values from 0 to 31, as said below
- block_count: int32 [32], P('group'), parts along dimension 0, may hold values from 6 to 12
- response_length: int32 [32], P(('group', 'seq')), parts along dimension 0, may hold values from 65 to 128
Outputs:
- output: bfloat16 [4096, 4096], P(('group', 'seq')), parts along dimension 0
- query_grad: bfloat16 [4096, 4096], P(('group', 'seq')), parts along dimension 0
- response_key_grad: bfloat16 [4096, 512], P(('group', 'seq')), parts along dimension 0
- response_value_grad: bfloat16 [4096, 512], P(('group', 'seq')), parts along dimension 0
- prompt_key_grad: bfloat16 [2048, 512], P(('group', 'seq')), parts along dimension 0
- prompt_value_grad: bfloat16 [2048, 512], P(('group', 'seq')), parts along dimension 0
The draws below stay inside these ranges and needn't reach their ends.
There are 2 independent parts, one for each index of `group`. The reference program is written for one: setup_inputs(seed, part) draws one part's arguments, and reference() takes and returns one part's arrays. A program takes and returns all parts, laid end to end along the dimension named above; each array names one. Nothing has to cross between parts.
Inputs may be any that keep to these rules, and one draw needn't show every extreme that they name: `block_list`: each row names 12 different prompt blocks and at most one of the two blocks 2 p and 2 p + 1 that device p holds; entries at or after block_count of the row name blocks too but are not read.
All inputs are finite; a program needn't handle non-finite values.
Results may differ from the reference program's by a relative error of at most 0.022.
Values may be sent and summed in bfloat16 or wider, within the bound.
A program may use at most 64 MiB of HBM per device.

```python
import math
import jax
import jax.numpy as jnp
from jax import lax

HD = 128
QH = 32
KVH = 4
RD = 128
BLK = 32
RESPONSES = 16
LMAX = 12
TOKR = 2048
PTOK = 1024


def draw_queries(key, part):
    key = jax.random.fold_in(key, 1)
    row_total = RESPONSES * RD
    values = jnp.clip(2.0 * jax.random.normal(key, (row_total, QH * HD), jnp.float32), -8.0, 8.0)
    return values.astype(jnp.bfloat16)


def draw_response_keys(key, part):
    key = jax.random.fold_in(key, 2)
    row_total = RESPONSES * RD
    values = jnp.clip(jax.random.normal(key, (row_total, KVH * HD), jnp.float32), -6.0, 6.0)
    return values.astype(jnp.bfloat16)


def draw_block_list(key, part):
    key = jax.random.fold_in(key, 3)
    first_key, second_key = jax.random.split(key)
    row_keys = jax.random.split(first_key, RESPONSES)
    owner_order = jax.vmap(lambda subkey: jax.random.permutation(subkey, RESPONSES))(row_keys)[:, :LMAX]
    halves = jax.random.randint(second_key, (RESPONSES, LMAX), 0, 2)
    return (2 * owner_order + halves).astype(jnp.int32)


def draw_block_count(key, part):
    key = jax.random.fold_in(key, 5)
    first_key, second_key = jax.random.split(key)
    counts = jax.random.randint(first_key, (RESPONSES,), LMAX // 2, LMAX + 1)
    chosen = jax.random.randint(second_key, (), 0, RESPONSES)
    rows_index = jnp.arange(RESPONSES)
    counts = jnp.where(rows_index == chosen, LMAX, counts)
    counts = jnp.where(rows_index == (chosen + 1) % RESPONSES, LMAX // 2, counts)
    return counts.astype(jnp.int32)


def draw_response_length(key, part):
    key = jax.random.fold_in(key, 7)
    first_key, second_key = jax.random.split(key)
    lengths = jax.random.randint(first_key, (RESPONSES,), RD // 2 + 1, RD + 1)
    chosen = jax.random.randint(second_key, (), 0, RESPONSES)
    rows_index = jnp.arange(RESPONSES)
    lengths = jnp.where(rows_index == chosen, RD, lengths)
    lengths = jnp.where(rows_index == (chosen + 1) % RESPONSES, RD // 2 + 1, lengths)
    return lengths.astype(jnp.int32)


def block_levels(key, shape, pieces, smallest, largest):
    gain, own = 1.0, jax.random.fold_in(key, 6)
    for dim, parts in pieces:
        steps = jnp.exp(jax.random.uniform(jax.random.fold_in(own, dim), (parts,), jnp.float32, smallest / len(pieces), largest / len(pieces)))
        gain = gain * jnp.repeat(steps, shape[dim] // parts).reshape([-1 if axis == dim else 1 for axis in range(len(shape))])
    return gain


def normal_values(key, dims, scale, limit, cuts=(), held_as=jnp.bfloat16):
    factor_of = block_levels(key, dims, cuts, -0.22, 0.18) if cuts else 1.0
    entries = jax.random.normal(key, dims, jnp.float32) * scale * factor_of
    return jnp.minimum(jnp.maximum(entries, -limit), limit).astype(held_as)


def setup_inputs(seed: int = 0, part: int = 0) -> dict:
    arg_keys = jax.random.split(jax.random.key(seed), 10)
    part_splits = jax.random.split(jax.random.fold_in(arg_keys[9], part), 10)
    queries = draw_queries(jax.random.fold_in(jax.random.fold_in(arg_keys[9], part), 71), part)
    response_keys = draw_response_keys(jax.random.fold_in(jax.random.fold_in(arg_keys[9], part), 71), part)
    response_values = normal_values(part_splits[2], (TOKR, KVH * HD), 1.0, 6.0, ((0, 16),))
    output_grad = normal_values(part_splits[3], (TOKR, QH * HD), 1.0, 6.0, ((0, 16),))
    prompt_keys = normal_values(part_splits[4], (PTOK, KVH * HD), 1.0, 6.0, ((0, 16),))
    prompt_values = normal_values(part_splits[5], (PTOK, KVH * HD), 1.0, 6.0, ((0, 16),))
    block_list = draw_block_list(jax.random.fold_in(jax.random.fold_in(arg_keys[9], part), 71), part)
    block_count = draw_block_count(jax.random.fold_in(jax.random.fold_in(arg_keys[9], part), 71), part)
    response_length = draw_response_length(jax.random.fold_in(jax.random.fold_in(arg_keys[9], part), 71), part)
    return dict(queries=queries, response_keys=response_keys, response_values=response_values, output_grad=output_grad, prompt_keys=prompt_keys, prompt_values=prompt_values, block_list=block_list, block_count=block_count, response_length=response_length)


masked_score = -1e+30

def rounded(values):
    return lax.optimization_barrier(values.astype(jnp.bfloat16)).astype(jnp.float32)

def reference(queries, response_keys, response_values, output_grad, prompt_keys, prompt_values, block_list, block_count, response_length):
    group_size = QH // KVH
    scaling = 1.0 / math.sqrt(HD)
    block_total = PTOK // BLK
    key_blocks = prompt_keys.reshape(block_total, BLK, KVH * HD)
    value_blocks = prompt_values.reshape(block_total, BLK, KVH * HD)
    positions = jnp.arange(RD)
    prefix_count = LMAX * BLK

    def response_step(sums, element):
        query_rows, own_keys, own_values, grad_rows, listed_ids, listed_count, live_length = element
        key_grad_sum, value_grad_sum = sums
        entry_live = jnp.arange(LMAX) < listed_count
        prefix_keys = jnp.take(key_blocks, listed_ids, axis=0).reshape(prefix_count, KVH * HD)
        prefix_values = jnp.take(value_blocks, listed_ids, axis=0).reshape(prefix_count, KVH * HD)
        keys_all = jnp.concatenate([prefix_keys, own_keys], 0).astype(jnp.float32).reshape(-1, KVH, HD)
        values_all = jnp.concatenate([prefix_values, own_values], 0).astype(jnp.float32).reshape(-1, KVH, HD)
        prefix_visible = jnp.broadcast_to(jnp.repeat(entry_live, BLK)[None, :], (RD, prefix_count))
        self_visible = (positions[None, :] <= positions[:, None]) & (positions[None, :] < live_length)
        visible = jnp.concatenate([prefix_visible, self_visible], 1)
        query_heads = query_rows.astype(jnp.float32).reshape(RD, KVH, group_size, HD)
        live_grad = jnp.where((positions < live_length)[:, None], grad_rows, jnp.zeros_like(grad_rows))
        grad_heads = live_grad.astype(jnp.float32).reshape(RD, KVH, group_size, HD)
        scores = jnp.einsum('tkgd,skd->kgts', query_heads, keys_all) * scaling
        scores = jnp.where(visible, scores, masked_score)
        row_max = scores.max(-1, keepdims=True)
        exponentials = jnp.exp(scores - row_max)
        weights = exponentials / exponentials.sum(-1, keepdims=True)
        weights_low = rounded(weights)
        output_heads = rounded(jnp.einsum('kgts,skd->tkgd', weights_low, values_all))
        delta = jnp.einsum('tkgd,tkgd->kgt', grad_heads, output_heads)
        weight_grad = jnp.einsum('tkgd,skd->kgts', grad_heads, values_all)
        score_grad = rounded(weights * (weight_grad - delta[..., None]) * scaling)
        query_grad = jnp.einsum('kgts,skd->tkgd', score_grad, keys_all)
        key_terms = jnp.einsum('kgts,tkgd->skd', score_grad, query_heads).reshape(-1, KVH * HD)
        value_terms = jnp.einsum('kgts,tkgd->skd', weights_low, grad_heads).reshape(-1, KVH * HD)
        key_grad_sum = key_grad_sum.at[listed_ids].add(rounded(key_terms[:prefix_count]).reshape(LMAX, BLK, KVH * HD))
        value_grad_sum = value_grad_sum.at[listed_ids].add(rounded(value_terms[:prefix_count]).reshape(LMAX, BLK, KVH * HD))
        results = (output_heads.reshape(RD, QH * HD).astype(jnp.bfloat16), query_grad.reshape(RD, QH * HD).astype(jnp.bfloat16), key_terms[prefix_count:].astype(jnp.bfloat16), value_terms[prefix_count:].astype(jnp.bfloat16))
        return ((key_grad_sum, value_grad_sum), results)
    initial = (jnp.zeros((block_total, BLK, KVH * HD), jnp.float32), jnp.zeros((block_total, BLK, KVH * HD), jnp.float32))
    inputs = (queries.reshape(RESPONSES, RD, QH * HD), response_keys.reshape(RESPONSES, RD, KVH * HD), response_values.reshape(RESPONSES, RD, KVH * HD), output_grad.reshape(RESPONSES, RD, QH * HD), block_list, block_count, response_length)
    sums, results = lax.scan(response_step, initial, inputs)
    output = results[0].reshape(TOKR, QH * HD)
    query_grad = results[1].reshape(TOKR, QH * HD)
    response_key_grad = results[2].reshape(TOKR, KVH * HD)
    response_value_grad = results[3].reshape(TOKR, KVH * HD)
    prompt_key_grad = sums[0].reshape(PTOK, KVH * HD).astype(jnp.bfloat16)
    prompt_value_grad = sums[1].reshape(PTOK, KVH * HD).astype(jnp.bfloat16)
    return (output, query_grad, response_key_grad, response_value_grad, prompt_key_grad, prompt_value_grad)
```

```python
import functools
import math

import jax
import jax.numpy as jnp
from jax import lax
from jax.experimental import pallas as pl
from jax.experimental.pallas import tpu as pltpu
from jax.sharding import PartitionSpec as P

HD = 128
QH = 32
KVH = 4
GROUP = QH // KVH

MASKED = -1e30


def dot(a, b, ca=1, cb=0):
    return lax.dot_general(
        a, b, (((ca,), (cb,)), ((), ())), preferred_element_type=jnp.float32
    )


def attention_kernel(
    block_rows,
    slots_ref,
    meta_ref,
    q_ref,
    do_ref,
    pk_ref,
    pv_ref,
    ok_ref,
    ov_ref,
    out_ref,
    dq_ref,
    dok_ref,
    dov_ref,
    dpk_ref,
    dpv_ref,
    k_all,
    v_all,
    bias,
    ds_all,
    wl_all,
    q_all,
    do_all,
):
    rows = q_ref.shape[0]
    entries = slots_ref.shape[0]
    prefix = entries * block_rows
    keys = prefix + rows
    scaling = 1.0 / math.sqrt(HD)
    count, length = meta_ref[0], meta_ref[1]

    @pl.when(pl.program_id(0) == 0)
    def _():
        key_row = lax.broadcasted_iota(jnp.int32, (prefix, 2 * rows), 0)
        bias[:prefix, :] = jnp.where(key_row < count * block_rows, 0.0, MASKED)
        own = lax.broadcasted_iota(jnp.int32, (rows, rows), 0)
        tok = lax.broadcasted_iota(jnp.int32, (rows, rows), 1)
        own_bias = jnp.where((own <= tok) & (own < length), 0.0, MASKED)
        bias[prefix:, :rows] = own_bias
        bias[prefix:, rows:] = own_bias

    for i in range(entries):
        start = pl.multiple_of(slots_ref[i] * block_rows, block_rows)
        k_all[i * block_rows : (i + 1) * block_rows, :] = pk_ref[pl.ds(start, block_rows), :]
        v_all[i * block_rows : (i + 1) * block_rows, :] = pv_ref[pl.ds(start, block_rows), :]
    k_all[prefix:, :] = ok_ref[...]
    v_all[prefix:, :] = ov_ref[...]
    kk, vv = k_all[...], v_all[...]
    kt, vt = kk.T, vv.T
    live = (lax.broadcasted_iota(jnp.int32, (rows, HD), 0) < length).astype(jnp.float32)
    live = live.astype(jnp.bfloat16)
    for h in range(GROUP):
        q_all[h * rows : (h + 1) * rows, :] = q_ref[:, h * HD : (h + 1) * HD]
        do_all[h * rows : (h + 1) * rows, :] = do_ref[:, h * HD : (h + 1) * HD] * live
    for pair in range(GROUP // 2):
        span = slice(pair * 2 * rows, (pair + 1) * 2 * rows)
        q2, do2 = q_all[span, :], do_all[span, :]
        do2t = do2.T
        s = dot(kk, q2, 1, 1) * (scaling * math.log2(math.e)) + bias[...]
        e = jnp.exp2(s - s.max(0, keepdims=True))
        w = e * (1.0 / e.sum(0, keepdims=True))
        wl = w.astype(jnp.bfloat16)
        wl_all[:, span] = wl
        ot = dot(vt, wl).astype(jnp.bfloat16)
        delta = (do2t.astype(jnp.float32) * ot.astype(jnp.float32)).sum(0, keepdims=True)
        dp = dot(vv, do2t)
        ds = (w * (dp - delta) * scaling).astype(jnp.bfloat16)
        ds_all[:, span] = ds
        dqt = dot(kt, ds).astype(jnp.bfloat16)
        for j in range(2):
            h = 2 * pair + j
            out_ref[:, h * HD : (h + 1) * HD] = ot[:, j * rows : (j + 1) * rows].T
            dq_ref[:, h * HD : (h + 1) * HD] = dqt[:, j * rows : (j + 1) * rows].T
    dk = dot(ds_all[...], q_all[...]).astype(jnp.bfloat16)
    dv = dot(wl_all[...], do_all[...]).astype(jnp.bfloat16)
    dok_ref[...] = dk[prefix:, :]
    dov_ref[...] = dv[prefix:, :]
    dpk_ref[...] = jnp.zeros_like(dpk_ref)
    dpv_ref[...] = jnp.zeros_like(dpv_ref)
    for i in range(entries):
        start = pl.multiple_of(slots_ref[i] * block_rows, block_rows)
        dpk_ref[pl.ds(start, block_rows), :] = dk[i * block_rows : (i + 1) * block_rows, :]
        dpv_ref[pl.ds(start, block_rows), :] = dv[i * block_rows : (i + 1) * block_rows, :]


def attention(slots, meta, queries, grads, keys, values, own_keys, own_values, block_rows):
    rows, width = queries.shape
    slot_rows = keys.shape[0]
    total = slots.shape[0] * block_rows + rows
    wide = pl.BlockSpec((rows, GROUP * HD), lambda g, *_: (0, g))
    own = pl.BlockSpec((rows, HD), lambda g, *_: (0, g))
    prompt = pl.BlockSpec((slot_rows, HD), lambda g, *_: (0, g))
    low = jnp.bfloat16
    return pl.pallas_call(
        functools.partial(attention_kernel, block_rows),
        grid_spec=pltpu.PrefetchScalarGridSpec(
            num_scalar_prefetch=2,
            grid=(KVH,),
            in_specs=[wide, wide, prompt, prompt, own, own],
            out_specs=[wide, wide, own, own, prompt, prompt],
            scratch_shapes=[
                pltpu.VMEM((total, HD), low),
                pltpu.VMEM((total, HD), low),
                pltpu.VMEM((total, 2 * rows), jnp.float32),
                pltpu.VMEM((total, GROUP * rows), low),
                pltpu.VMEM((total, GROUP * rows), low),
                pltpu.VMEM((GROUP * rows, HD), low),
                pltpu.VMEM((GROUP * rows, HD), low),
            ],
        ),
        out_shape=[
            jax.ShapeDtypeStruct((rows, width), low),
            jax.ShapeDtypeStruct((rows, width), low),
            jax.ShapeDtypeStruct((rows, KVH * HD), low),
            jax.ShapeDtypeStruct((rows, KVH * HD), low),
            jax.ShapeDtypeStruct((slot_rows, KVH * HD), low),
            jax.ShapeDtypeStruct((slot_rows, KVH * HD), low),
        ],
        compiler_params=pltpu.CompilerParams(vmem_limit_bytes=40 << 20),
        name="attention",
    )(slots, meta, queries, grads, keys, values, own_keys, own_values)


def per_device(
    queries,
    response_keys,
    response_values,
    output_grad,
    prompt_keys,
    prompt_values,
    block_list,
    block_count,
    response_length,
):
    device_index = lax.axis_index("seq")
    listed = lax.dynamic_index_in_dim(block_list, device_index, 0, keepdims=False)
    count = lax.dynamic_index_in_dim(block_count, device_index, 0, keepdims=True)
    meta = jnp.concatenate([count, response_length])
    block_rows = prompt_keys.shape[0] // 2
    all_keys = lax.all_gather(prompt_keys, "seq", axis=0, tiled=True)
    all_values = lax.all_gather(prompt_values, "seq", axis=0, tiled=True)
    out, dq, dok, dov, dpk, dpv = attention(
        listed, meta, queries, output_grad, all_keys, all_values, response_keys, response_values, block_rows
    )
    return (
        out,
        dq,
        dok,
        dov,
        lax.psum_scatter(dpk, "seq", scatter_dimension=0, tiled=True),
        lax.psum_scatter(dpv, "seq", scatter_dimension=0, tiled=True),
    )


def solution(mesh):
    both = P(("group", "seq"), None)
    return jax.shard_map(
        per_device,
        mesh=mesh,
        in_specs=(both, both, both, both, both, both, P("group", None), P("group"), P(("group", "seq"))),
        out_specs=(both,) * 6,
        check_vma=False,
    )
```

```python
import functools
import math

import jax
import jax.numpy as jnp
from jax import lax
from jax.experimental import pallas as pl
from jax.experimental.pallas import tpu as pltpu
from jax.sharding import PartitionSpec as P

HD = 128
QH = 32
KVH = 4
GROUP = QH // KVH

MASKED = -1e30


def dot(a, b, ca=1, cb=0):
    return lax.dot_general(
        a, b, (((ca,), (cb,)), ((), ())), preferred_element_type=jnp.float32
    )


def attention_kernel(
    block_rows,
    slots_ref,
    meta_ref,
    q_ref,
    do_ref,
    pkv_ref,
    ok_ref,
    ov_ref,
    out_ref,
    dq_ref,
    dok_ref,
    dov_ref,
    dpkv_ref,
    k_all,
    v_all,
    bias,
    ds_all,
    wl_all,
    q_all,
    do_all,
):
    rows = q_ref.shape[0]
    entries = slots_ref.shape[0]
    prefix = entries * block_rows
    keys = prefix + rows
    scaling = 1.0 / math.sqrt(HD)
    count, length = meta_ref[0], meta_ref[1]

    @pl.when(pl.program_id(0) == 0)
    def _():
        key_row = lax.broadcasted_iota(jnp.int32, (prefix, 2 * rows), 0)
        bias[:prefix, :] = jnp.where(key_row < count * block_rows, 0.0, MASKED)
        own = lax.broadcasted_iota(jnp.int32, (rows, rows), 0)
        tok = lax.broadcasted_iota(jnp.int32, (rows, rows), 1)
        own_bias = jnp.where((own <= tok) & (own < length), 0.0, MASKED)
        bias[prefix:, :rows] = own_bias
        bias[prefix:, rows:] = own_bias

    for i in range(entries):
        start = pl.multiple_of(slots_ref[i] * block_rows, block_rows)
        k_all[i * block_rows : (i + 1) * block_rows, :] = pkv_ref[pl.ds(start, block_rows), :HD]
        v_all[i * block_rows : (i + 1) * block_rows, :] = pkv_ref[pl.ds(start, block_rows), HD:]
    k_all[prefix:, :] = ok_ref[...]
    v_all[prefix:, :] = ov_ref[...]
    kk, vv = k_all[...], v_all[...]
    kt, vt = kk.T, vv.T
    live = (lax.broadcasted_iota(jnp.int32, (rows, HD), 0) < length).astype(jnp.float32)
    live = live.astype(jnp.bfloat16)
    for h in range(GROUP):
        q_all[h * rows : (h + 1) * rows, :] = q_ref[:, h * HD : (h + 1) * HD]
        do_all[h * rows : (h + 1) * rows, :] = do_ref[:, h * HD : (h + 1) * HD] * live
    for pair in range(GROUP // 2):
        span = slice(pair * 2 * rows, (pair + 1) * 2 * rows)
        q2, do2 = q_all[span, :], do_all[span, :]
        do2t = do2.T
        s = dot(kk, q2, 1, 1) * (scaling * math.log2(math.e)) + bias[...]
        e = jnp.exp2(s - s.max(0, keepdims=True))
        w = e * (1.0 / e.sum(0, keepdims=True))
        wl = w.astype(jnp.bfloat16)
        wl_all[:, span] = wl
        ot = dot(vt, wl).astype(jnp.bfloat16)
        delta = (do2t.astype(jnp.float32) * ot.astype(jnp.float32)).sum(0, keepdims=True)
        dp = dot(vv, do2t)
        ds = (w * (dp - delta) * scaling).astype(jnp.bfloat16)
        ds_all[:, span] = ds
        dqt = dot(kt, ds).astype(jnp.bfloat16)
        for j in range(2):
            h = 2 * pair + j
            out_ref[:, h * HD : (h + 1) * HD] = ot[:, j * rows : (j + 1) * rows].T
            dq_ref[:, h * HD : (h + 1) * HD] = dqt[:, j * rows : (j + 1) * rows].T
    dk = dot(ds_all[...], q_all[...]).astype(jnp.bfloat16)
    dv = dot(wl_all[...], do_all[...]).astype(jnp.bfloat16)
    dok_ref[...] = dk[prefix:, :]
    dov_ref[...] = dv[prefix:, :]
    dpkv_ref[...] = jnp.zeros_like(dpkv_ref)
    for i in range(entries):
        start = pl.multiple_of(slots_ref[i] * block_rows, block_rows)
        dpkv_ref[pl.ds(start, block_rows), :HD] = dk[i * block_rows : (i + 1) * block_rows, :]
        dpkv_ref[pl.ds(start, block_rows), HD:] = dv[i * block_rows : (i + 1) * block_rows, :]


def attention(slots, meta, queries, grads, prompt, own_keys, own_values, block_rows):
    rows, width = queries.shape
    slot_rows = prompt.shape[0]
    total = slots.shape[0] * block_rows + rows
    wide = pl.BlockSpec((rows, GROUP * HD), lambda g, *_: (0, g))
    own = pl.BlockSpec((rows, HD), lambda g, *_: (0, g))
    shared = pl.BlockSpec((slot_rows, 2 * HD), lambda g, *_: (0, g))
    low = jnp.bfloat16
    return pl.pallas_call(
        functools.partial(attention_kernel, block_rows),
        grid_spec=pltpu.PrefetchScalarGridSpec(
            num_scalar_prefetch=2,
            grid=(KVH,),
            in_specs=[wide, wide, shared, own, own],
            out_specs=[wide, wide, own, own, shared],
            scratch_shapes=[
                pltpu.VMEM((total, HD), low),
                pltpu.VMEM((total, HD), low),
                pltpu.VMEM((total, 2 * rows), jnp.float32),
                pltpu.VMEM((total, GROUP * rows), low),
                pltpu.VMEM((total, GROUP * rows), low),
                pltpu.VMEM((GROUP * rows, HD), low),
                pltpu.VMEM((GROUP * rows, HD), low),
            ],
        ),
        out_shape=[
            jax.ShapeDtypeStruct((rows, width), low),
            jax.ShapeDtypeStruct((rows, width), low),
            jax.ShapeDtypeStruct((rows, KVH * HD), low),
            jax.ShapeDtypeStruct((rows, KVH * HD), low),
            jax.ShapeDtypeStruct((slot_rows, 2 * KVH * HD), low),
        ],
        compiler_params=pltpu.CompilerParams(vmem_limit_bytes=56 << 20),
        name="attention",
    )(slots, meta, queries, grads, prompt, own_keys, own_values)


MESH = pl.DeviceIdType.MESH


def plane(n):
    me = lax.axis_index("seq")
    z, y, c = me // 4, lax.rem(me // 2, 2), lax.rem(me, 2)

    def index(dz, y, c):
        return lax.rem(z + dz + n // 4, n // 4) * 4 + y * 2 + c

    return me, y, c, index


def greet(peers):
    barrier = pltpu.get_barrier_semaphore()
    for peer in peers:
        pl.semaphore_signal(barrier, inc=1, device_id={"seq": peer}, device_id_type=MESH)
    pl.semaphore_wait(barrier, len(peers))


def gather_kernel(n, k_ref, v_ref, all_ref, zs, zr, ys, yr, cs, cr):
    me, y, c, index = plane(n)
    nz = n // 4
    size = k_ref.shape[0]

    def at(source):
        return all_ref.at[pl.ds(pl.multiple_of(source * size, size), size), :]

    for g in range(KVH):
        all_ref[pl.ds(pl.multiple_of(me * size, size), size), 2 * g * HD : (2 * g + 1) * HD] = k_ref[
            :, g * HD : (g + 1) * HD
        ]
        all_ref[pl.ds(pl.multiple_of(me * size, size), size), (2 * g + 1) * HD : (2 * g + 2) * HD] = v_ref[
            :, g * HD : (g + 1) * HD
        ]
    across, partner = index(0, 1 - y, c), index(0, y, 1 - c)
    greet([index(dz, y, c) for dz in range(1, nz)] + [across, partner])

    def copy(source, send, recv, peer):
        return pltpu.make_async_remote_copy(
            src_ref=at(source),
            dst_ref=at(source),
            send_sem=send,
            recv_sem=recv,
            device_id={"seq": peer},
            device_id_type=MESH,
        )

    started = []

    def start(*args):
        started.append(copy(*args))
        started[-1].start()

    for dz in range(1, nz):
        start(me, zs.at[dz], zr.at[dz], index(dz, y, c))
    for dz in range(nz):
        source = index(-dz, y, c)
        if dz:
            copy(source, zs.at[dz], zr.at[dz], across).wait_recv()
        start(source, ys.at[dz], yr.at[dz], across)
        start(source, cs.at[dz], cr.at[dz], partner)
    for dz in range(nz):
        source = index(-dz, 1 - y, c)
        copy(source, ys.at[dz], yr.at[dz], across).wait_recv()
        start(source, cs.at[nz + dz], cr.at[nz + dz], partner)
    for dz in range(nz):
        copy(index(-dz, y, 1 - c), cs.at[dz], cr.at[dz], partner).wait_recv()
        copy(index(-dz, 1 - y, 1 - c), cs.at[nz + dz], cr.at[nz + dz], partner).wait_recv()
    for one in started:
        one.wait_send()


def gather(keys, values, n):
    rows, width = keys.shape
    nz = n // 4
    vmem = pl.BlockSpec(memory_space=pltpu.VMEM)
    dma = pltpu.SemaphoreType.DMA
    return pl.pallas_call(
        functools.partial(gather_kernel, n),
        in_specs=[vmem, vmem],
        out_specs=vmem,
        out_shape=jax.ShapeDtypeStruct((n * rows, 2 * width), keys.dtype),
        scratch_shapes=[dma((nz,)), dma((nz,)), dma((nz,)), dma((nz,)), dma((2 * nz,)), dma((2 * nz,))],
        compiler_params=pltpu.CompilerParams(
            collective_id=0, has_side_effects=True, vmem_limit_bytes=24 << 20
        ),
        name="gather",
    )(keys, values)


def scatter_kernel(n, t_ref, pk_ref, pv_ref, crecv, yrecv, zrecv, ysend, zsend, cs, cr, ys, yr, zs, zr):
    me, y, c, index = plane(n)
    nz = n // 4
    size = pk_ref.shape[0]
    across, partner = index(0, 1 - y, c), index(0, y, 1 - c)

    def at(owner):
        return t_ref.at[pl.ds(pl.multiple_of(owner * size, size), size), :]

    def copy(source, target, send, recv, peer):
        return pltpu.make_async_remote_copy(
            src_ref=source,
            dst_ref=target,
            send_sem=send,
            recv_sem=recv,
            device_id={"seq": peer},
            device_id_type=MESH,
        )

    greet([index(dz, y, c) for dz in range(1, nz)] + [across, partner])
    order = list(range(1, nz)) + [0]
    inside, over, along = {}, {}, {}
    for dz in order:
        for far in (1, 0):
            slot = 2 * dz + far
            owner = index(dz, 1 - y if far else y, 1 - c)
            inside[slot] = copy(at(owner), crecv.at[slot], cs.at[slot], cr.at[slot], partner)
            inside[slot].start()
    for dz in order:
        inside[2 * dz + 1].wait_recv()
        mine = at(index(dz, 1 - y, c))[...].astype(jnp.float32)
        ysend[dz] = (mine + crecv[2 * dz + 1].astype(jnp.float32)).astype(ysend.dtype)
        over[dz] = copy(ysend.at[dz], yrecv.at[dz], ys.at[dz], yr.at[dz], across)
        over[dz].start()
    total = None
    for dz in order:
        inside[2 * dz].wait_recv()
        mine = at(index(dz, y, c))[...].astype(jnp.float32) + crecv[2 * dz].astype(jnp.float32)
        over[dz].wait_recv()
        mine = mine + yrecv[dz].astype(jnp.float32)
        if dz:
            zsend[dz] = mine.astype(zsend.dtype)
            along[dz] = copy(zsend.at[dz], zrecv.at[dz], zs.at[dz], zr.at[dz], index(dz, y, c))
            along[dz].start()
        else:
            total = mine
    for dz in range(1, nz):
        along[dz].wait_recv()
        total = total + zrecv[dz].astype(jnp.float32)
    total = total.astype(pk_ref.dtype)
    for g in range(KVH):
        pk_ref[:, g * HD : (g + 1) * HD] = total[:, 2 * g * HD : (2 * g + 1) * HD]
        pv_ref[:, g * HD : (g + 1) * HD] = total[:, (2 * g + 1) * HD : (2 * g + 2) * HD]
    for one in [*inside.values(), *over.values(), *along.values()]:
        one.wait_send()


def scatter(terms, n):
    rows, width = terms.shape[0] // n, terms.shape[1]
    nz = n // 4
    vmem = pl.BlockSpec(memory_space=pltpu.VMEM)
    dma = pltpu.SemaphoreType.DMA
    block = (nz, rows, width)
    low = terms.dtype
    return pl.pallas_call(
        functools.partial(scatter_kernel, n),
        in_specs=[vmem],
        out_specs=[vmem, vmem],
        out_shape=[jax.ShapeDtypeStruct((rows, width // 2), low)] * 2,
        scratch_shapes=[
            pltpu.VMEM((2 * nz, rows, width), low),
            pltpu.VMEM(block, low),
            pltpu.VMEM(block, low),
            pltpu.VMEM(block, low),
            pltpu.VMEM(block, low),
            dma((2 * nz,)),
            dma((2 * nz,)),
            dma((nz,)),
            dma((nz,)),
            dma((nz,)),
            dma((nz,)),
        ],
        compiler_params=pltpu.CompilerParams(
            collective_id=1, has_side_effects=True, vmem_limit_bytes=40 << 20
        ),
        name="scatter",
    )(terms)


def per_device(
    queries,
    response_keys,
    response_values,
    output_grad,
    prompt_keys,
    prompt_values,
    block_list,
    block_count,
    response_length,
):
    device_index = lax.axis_index("seq")
    listed = lax.dynamic_index_in_dim(block_list, device_index, 0, keepdims=False)
    count = lax.dynamic_index_in_dim(block_count, device_index, 0, keepdims=True)
    meta = jnp.concatenate([count, response_length])
    block_rows = prompt_keys.shape[0] // 2
    n = lax.axis_size("seq")
    prompt = gather(prompt_keys, prompt_values, n)
    out, dq, dok, dov, terms = attention(
        listed, meta, queries, output_grad, prompt, response_keys, response_values, block_rows
    )
    dpk, dpv = scatter(terms, n)
    return out, dq, dok, dov, dpk, dpv


def solution(mesh):
    both = P(("group", "seq"), None)
    return jax.shard_map(
        per_device,
        mesh=mesh,
        in_specs=(both, both, both, both, both, both, P("group", None), P("group"), P(("group", "seq"))),
        out_specs=(both,) * 6,
        check_vma=False,
    )
```

```python
import functools
import math

import jax
import jax.numpy as jnp
from jax import lax
from jax.experimental import pallas as pl
from jax.experimental.pallas import tpu as pltpu
from jax.sharding import PartitionSpec as P

HD = 128
QH = 32
KVH = 4
GROUP = QH // KVH

PARTS = 2
MASKED = -1e30


def dot(a, b, ca=1, cb=0):
    return lax.dot_general(
        a, b, (((ca,), (cb,)), ((), ())), preferred_element_type=jnp.float32
    )


def attention_kernel(
    block_rows,
    list_ref,
    count_ref,
    length_ref,
    q_ref,
    do_ref,
    pkv_ref,
    ok_ref,
    ov_ref,
    out_ref,
    dq_ref,
    dok_ref,
    dov_ref,
    dpkv_ref,
    k_all,
    v_all,
    bias,
    ds_all,
    wl_all,
    q_all,
    do_all,
):
    rows = q_ref.shape[0]
    entries = list_ref.shape[1]
    me = lax.axis_index("seq")
    g = pl.program_id(0)
    key_cols = pl.ds(pl.multiple_of(g * HD, HD), HD)
    value_cols = pl.ds(pl.multiple_of((KVH + g) * HD, HD), HD)
    prefix = entries * block_rows
    keys = prefix + rows
    scaling = 1.0 / math.sqrt(HD)
    count, length = count_ref[me], length_ref[0]

    @pl.when(g == 0)
    def _():
        key_row = lax.broadcasted_iota(jnp.int32, (prefix, 2 * rows), 0)
        bias[:prefix, :] = jnp.where(key_row < count * block_rows, 0.0, MASKED)
        own = lax.broadcasted_iota(jnp.int32, (rows, rows), 0)
        tok = lax.broadcasted_iota(jnp.int32, (rows, rows), 1)
        own_bias = jnp.where((own <= tok) & (own < length), 0.0, MASKED)
        bias[prefix:, :rows] = own_bias
        bias[prefix:, rows:] = own_bias
        dpkv_ref[...] = jnp.zeros_like(dpkv_ref)

    for i in range(entries):
        start = pl.multiple_of(list_ref[me, i] * block_rows, block_rows)
        k_all[i * block_rows : (i + 1) * block_rows, :] = pkv_ref[pl.ds(start, block_rows), key_cols]
        v_all[i * block_rows : (i + 1) * block_rows, :] = pkv_ref[pl.ds(start, block_rows), value_cols]
    k_all[prefix:, :] = ok_ref[...]
    v_all[prefix:, :] = ov_ref[...]
    kk, vv = k_all[...], v_all[...]
    kt, vt = kk.T, vv.T
    live = (lax.broadcasted_iota(jnp.int32, (rows, HD), 0) < length).astype(jnp.float32)
    live = live.astype(jnp.bfloat16)
    for h in range(GROUP):
        q_all[h * rows : (h + 1) * rows, :] = q_ref[:, h * HD : (h + 1) * HD]
        do_all[h * rows : (h + 1) * rows, :] = do_ref[:, h * HD : (h + 1) * HD] * live
    for pair in range(GROUP // 2):
        span = slice(pair * 2 * rows, (pair + 1) * 2 * rows)
        q2, do2 = q_all[span, :], do_all[span, :]
        do2t = do2.T
        s = dot(kk, q2, 1, 1) * (scaling * math.log2(math.e)) + bias[...]
        e = jnp.exp2(s - s.max(0, keepdims=True))
        w = e * (1.0 / e.sum(0, keepdims=True))
        wl = w.astype(jnp.bfloat16)
        wl_all[:, span] = wl
        ot = dot(vt, wl).astype(jnp.bfloat16)
        delta = (do2t.astype(jnp.float32) * ot.astype(jnp.float32)).sum(0, keepdims=True)
        dp = dot(vv, do2t)
        ds = (w * (dp - delta) * scaling).astype(jnp.bfloat16)
        ds_all[:, span] = ds
        dqt = dot(kt, ds).astype(jnp.bfloat16)
        for j in range(2):
            h = 2 * pair + j
            out_ref[:, h * HD : (h + 1) * HD] = ot[:, j * rows : (j + 1) * rows].T
            dq_ref[:, h * HD : (h + 1) * HD] = dqt[:, j * rows : (j + 1) * rows].T
    dk = dot(ds_all[...], q_all[...]).astype(jnp.bfloat16)
    dv = dot(wl_all[...], do_all[...]).astype(jnp.bfloat16)
    dok_ref[...] = dk[prefix:, :]
    dov_ref[...] = dv[prefix:, :]
    for i in range(entries):
        start = pl.multiple_of(list_ref[me, i] * block_rows, block_rows)
        dpkv_ref[pl.ds(start, block_rows), key_cols] = dk[i * block_rows : (i + 1) * block_rows, :]
        dpkv_ref[pl.ds(start, block_rows), value_cols] = dv[i * block_rows : (i + 1) * block_rows, :]


def attention(block_list, block_count, length, queries, grads, prompt, own_keys, own_values, block_rows):
    rows, width = queries.shape
    slot_rows = prompt.shape[0]
    total = block_list.shape[1] * block_rows + rows
    wide = pl.BlockSpec((rows, GROUP * HD), lambda g, *_: (0, g))
    own = pl.BlockSpec((rows, HD), lambda g, *_: (0, g))
    shared = pl.BlockSpec(memory_space=pltpu.VMEM)
    low = jnp.bfloat16
    return pl.pallas_call(
        functools.partial(attention_kernel, block_rows),
        grid_spec=pltpu.PrefetchScalarGridSpec(
            num_scalar_prefetch=3,
            grid=(KVH,),
            in_specs=[wide, wide, shared, own, own],
            out_specs=[wide, wide, own, own, shared],
            scratch_shapes=[
                pltpu.VMEM((total, HD), low),
                pltpu.VMEM((total, HD), low),
                pltpu.VMEM((total, 2 * rows), jnp.float32),
                pltpu.VMEM((total, GROUP * rows), low),
                pltpu.VMEM((total, GROUP * rows), low),
                pltpu.VMEM((GROUP * rows, HD), low),
                pltpu.VMEM((GROUP * rows, HD), low),
            ],
        ),
        out_shape=[
            jax.ShapeDtypeStruct((rows, width), low),
            jax.ShapeDtypeStruct((rows, width), low),
            jax.ShapeDtypeStruct((rows, KVH * HD), low),
            jax.ShapeDtypeStruct((rows, KVH * HD), low),
            jax.ShapeDtypeStruct((slot_rows, 2 * KVH * HD), low),
        ],
        compiler_params=pltpu.CompilerParams(vmem_limit_bytes=(40 << 20) - 4 * prompt.size),
        name="attention",
    )(block_list, block_count, length, queries, grads, prompt, own_keys, own_values)


MESH = pl.DeviceIdType.MESH


def plane(n):
    me = lax.axis_index("seq")
    z, y, c = me // 4, lax.rem(me // 2, 2), lax.rem(me, 2)

    def index(dz, y, c):
        return lax.rem(z + dz + n // 4, n // 4) * 4 + y * 2 + c

    return me, y, c, index


def greet(peers):
    barrier = pltpu.get_barrier_semaphore()
    for peer in peers:
        pl.semaphore_signal(barrier, inc=1, device_id={"seq": peer}, device_id_type=MESH)
    pl.semaphore_wait(barrier, len(peers))


def gather_kernel(n, parts, k_ref, v_ref, all_ref, own_sem, zs, zr, ys, yr, cs, cr):
    me, y, c, index = plane(n)
    nz = n // 4
    size, width = k_ref.shape
    step = size // parts

    def at(source, part):
        return all_ref.at[pl.ds(pl.multiple_of(source * size + part * step, step), step), :]

    mine = pl.ds(pl.multiple_of(me * size, size), size)
    loads = [
        pltpu.make_async_copy(k_ref, all_ref.at[mine, :width], own_sem.at[0]),
        pltpu.make_async_copy(v_ref, all_ref.at[mine, width:], own_sem.at[1]),
    ]
    for one in loads:
        one.start()
    across, partner = index(0, 1 - y, c), index(0, y, 1 - c)
    greet([index(dz, y, c) for dz in range(1, nz)] + [across, partner])
    for one in loads:
        one.wait()

    def copy(source, part, send, recv, slot, peer):
        return pltpu.make_async_remote_copy(
            src_ref=at(source, part),
            dst_ref=at(source, part),
            send_sem=send.at[slot * parts + part],
            recv_sem=recv.at[slot * parts + part],
            device_id={"seq": peer},
            device_id_type=MESH,
        )

    started = []

    def start(*args):
        started.append(copy(*args))
        started[-1].start()

    for part in range(parts):
        for dz in range(1, nz):
            start(me, part, zs, zr, dz, index(dz, y, c))
        start(me, part, ys, yr, 0, across)
        start(me, part, cs, cr, 0, partner)

    def over(dz, part):
        source = index(-dz, 1 - y, c)
        copy(source, part, ys, yr, dz, across).wait_recv()
        start(source, part, cs, cr, nz + dz, partner)

    pending = []
    for part in range(parts):
        for dz in range(1, nz):
            source = index(-dz, y, c)
            copy(source, part, zs, zr, dz, across).wait_recv()
            start(source, part, ys, yr, dz, across)
            start(source, part, cs, cr, dz, partner)
        for one in pending:
            over(*one)
        pending = [(dz, part) for dz in range(1, nz)] + [(0, part)]
    for one in pending:
        over(*one)
    for part in range(parts):
        for dz in range(nz):
            copy(index(-dz, y, 1 - c), part, cs, cr, dz, partner).wait_recv()
            copy(index(-dz, 1 - y, 1 - c), part, cs, cr, nz + dz, partner).wait_recv()
    for one in started:
        one.wait_send()


def gather(keys, values, n):
    rows, width = keys.shape
    nz = n // 4
    vmem = pl.BlockSpec(memory_space=pltpu.VMEM)
    dma = pltpu.SemaphoreType.DMA
    parts = math.gcd(rows // 16, PARTS)
    some, more = dma((parts * nz,)), dma((parts * 2 * nz,))
    return pl.pallas_call(
        functools.partial(gather_kernel, n, parts),
        in_specs=[pl.BlockSpec(memory_space=pl.ANY)] * 2,
        out_specs=vmem,
        out_shape=jax.ShapeDtypeStruct((n * rows, 2 * width), keys.dtype),
        scratch_shapes=[dma((2,)), some, some, some, some, more, more],
        compiler_params=pltpu.CompilerParams(
            collective_id=0, has_side_effects=True, vmem_limit_bytes=(50 << 20) - 4 * n * rows * width
        ),
        name="gather",
    )(keys, values)


def scatter_kernel(n, t_ref, pk_ref, pv_ref, crecv, yrecv, zrecv, ysend, zsend, cs, cr, ys, yr, zs, zr):
    me, y, c, index = plane(n)
    nz = n // 4
    size = pk_ref.shape[0]
    across, partner = index(0, 1 - y, c), index(0, y, 1 - c)

    def at(owner):
        return t_ref.at[pl.ds(pl.multiple_of(owner * size, size), size), :]

    def copy(source, target, send, recv, peer):
        return pltpu.make_async_remote_copy(
            src_ref=source,
            dst_ref=target,
            send_sem=send,
            recv_sem=recv,
            device_id={"seq": peer},
            device_id_type=MESH,
        )

    greet([index(dz, y, c) for dz in range(1, nz)] + [across, partner])
    order = list(range(1, nz)) + [0]
    inside, over, along = {}, {}, {}
    for dz in order:
        for far in (1, 0):
            slot = 2 * dz + far
            owner = index(dz, 1 - y if far else y, 1 - c)
            inside[slot] = copy(at(owner), crecv.at[slot], cs.at[slot], cr.at[slot], partner)
            inside[slot].start()
    for dz in order:
        inside[2 * dz + 1].wait_recv()
        mine = at(index(dz, 1 - y, c))[...].astype(jnp.float32)
        ysend[dz] = (mine + crecv[2 * dz + 1].astype(jnp.float32)).astype(ysend.dtype)
        over[dz] = copy(ysend.at[dz], yrecv.at[dz], ys.at[dz], yr.at[dz], across)
        over[dz].start()
    total = None
    for dz in order:
        inside[2 * dz].wait_recv()
        mine = at(index(dz, y, c))[...].astype(jnp.float32) + crecv[2 * dz].astype(jnp.float32)
        over[dz].wait_recv()
        mine = mine + yrecv[dz].astype(jnp.float32)
        if dz:
            zsend[dz] = mine.astype(zsend.dtype)
            along[dz] = copy(zsend.at[dz], zrecv.at[dz], zs.at[dz], zr.at[dz], index(dz, y, c))
            along[dz].start()
        else:
            total = mine
    for dz in range(1, nz):
        along[dz].wait_recv()
        total = total + zrecv[dz].astype(jnp.float32)
    total = total.astype(pk_ref.dtype)
    pk_ref[...] = total[:, : pk_ref.shape[1]]
    pv_ref[...] = total[:, pk_ref.shape[1] :]
    for one in [*inside.values(), *over.values(), *along.values()]:
        one.wait_send()


def scatter(terms, n):
    rows, width = terms.shape[0] // n, terms.shape[1]
    nz = n // 4
    vmem = pl.BlockSpec(memory_space=pltpu.VMEM)
    dma = pltpu.SemaphoreType.DMA
    block = (nz, rows, width)
    low = terms.dtype
    return pl.pallas_call(
        functools.partial(scatter_kernel, n),
        in_specs=[vmem],
        out_specs=[vmem, vmem],
        out_shape=[jax.ShapeDtypeStruct((rows, width // 2), low)] * 2,
        scratch_shapes=[
            pltpu.VMEM((2 * nz, rows, width), low),
            pltpu.VMEM(block, low),
            pltpu.VMEM(block, low),
            pltpu.VMEM(block, low),
            pltpu.VMEM(block, low),
            dma((2 * nz,)),
            dma((2 * nz,)),
            dma((nz,)),
            dma((nz,)),
            dma((nz,)),
            dma((nz,)),
        ],
        compiler_params=pltpu.CompilerParams(
            collective_id=1, has_side_effects=True, vmem_limit_bytes=40 << 20
        ),
        name="scatter",
    )(terms)


def per_device(
    queries,
    response_keys,
    response_values,
    output_grad,
    prompt_keys,
    prompt_values,
    block_list,
    block_count,
    response_length,
):
    block_rows = prompt_keys.shape[0] // 2
    n = lax.axis_size("seq")
    prompt = gather(prompt_keys, prompt_values, n)
    out, dq, dok, dov, terms = attention(
        block_list,
        block_count,
        response_length,
        queries,
        output_grad,
        prompt,
        response_keys,
        response_values,
        block_rows,
    )
    dpk, dpv = scatter(terms, n)
    return out, dq, dok, dov, dpk, dpv


def solution(mesh):
    both = P(("group", "seq"), None)
    return jax.shard_map(
        per_device,
        mesh=mesh,
        in_specs=(both, both, both, both, both, both, P("group", None), P("group"), P(("group", "seq"))),
        out_specs=(both,) * 6,
        check_vma=False,
    )
```

```python
import functools
import math

import jax
import jax.numpy as jnp
from jax import lax
from jax.experimental import pallas as pl
from jax.experimental.pallas import tpu as pltpu
from jax.sharding import PartitionSpec as P

HD = 128
QH = 32
KVH = 4
GROUP = QH // KVH

PARTS = 4
MASKED = -1e30


def dot(a, b, ca=1, cb=0):
    return lax.dot_general(
        a, b, (((ca,), (cb,)), ((), ())), preferred_element_type=jnp.float32
    )


def attention_kernel(
    block_rows,
    list_ref,
    count_ref,
    length_ref,
    q_ref,
    do_ref,
    pkv_ref,
    ok_ref,
    ov_ref,
    out_ref,
    dq_ref,
    dok_ref,
    dov_ref,
    dpkv_ref,
    k_all,
    v_all,
    bias,
    ds_all,
    wl_all,
    q_all,
    do_all,
):
    rows = q_ref.shape[0]
    entries = list_ref.shape[1]
    me = lax.axis_index("seq")
    g = pl.program_id(0)
    key_cols = pl.ds(pl.multiple_of(g * HD, HD), HD)
    value_cols = pl.ds(pl.multiple_of((KVH + g) * HD, HD), HD)
    prefix = entries * block_rows
    keys = prefix + rows
    scaling = 1.0 / math.sqrt(HD)
    count, length = count_ref[me], length_ref[0]

    @pl.when(g == 0)
    def _():
        key_row = lax.broadcasted_iota(jnp.int32, (prefix, 2 * rows), 0)
        bias[:prefix, :] = jnp.where(key_row < count * block_rows, 0.0, MASKED)
        own = lax.broadcasted_iota(jnp.int32, (rows, rows), 0)
        tok = lax.broadcasted_iota(jnp.int32, (rows, rows), 1)
        own_bias = jnp.where((own <= tok) & (own < length), 0.0, MASKED)
        bias[prefix:, :rows] = own_bias
        bias[prefix:, rows:] = own_bias
        dpkv_ref[...] = jnp.zeros_like(dpkv_ref)

    for i in range(entries):
        start = pl.multiple_of(list_ref[me, i] * block_rows, block_rows)
        k_all[i * block_rows : (i + 1) * block_rows, :] = pkv_ref[pl.ds(start, block_rows), key_cols]
        v_all[i * block_rows : (i + 1) * block_rows, :] = pkv_ref[pl.ds(start, block_rows), value_cols]
    k_all[prefix:, :] = ok_ref[...]
    v_all[prefix:, :] = ov_ref[...]
    kk, vv = k_all[...], v_all[...]
    kt, vt = kk.T, vv.T
    live = (lax.broadcasted_iota(jnp.int32, (rows, HD), 0) < length).astype(jnp.float32)
    live = live.astype(jnp.bfloat16)
    for h in range(GROUP):
        q_all[h * rows : (h + 1) * rows, :] = q_ref[:, h * HD : (h + 1) * HD]
        do_all[h * rows : (h + 1) * rows, :] = do_ref[:, h * HD : (h + 1) * HD] * live
    for pair in range(GROUP // 2):
        span = slice(pair * 2 * rows, (pair + 1) * 2 * rows)
        q2, do2 = q_all[span, :], do_all[span, :]
        do2t = do2.T
        s = dot(kk, q2, 1, 1) * (scaling * math.log2(math.e)) + bias[...]
        e = jnp.exp2(s - s.max(0, keepdims=True))
        w = e * (1.0 / e.sum(0, keepdims=True))
        wl = w.astype(jnp.bfloat16)
        wl_all[:, span] = wl
        ot = dot(vt, wl).astype(jnp.bfloat16)
        delta = (do2t.astype(jnp.float32) * ot.astype(jnp.float32)).sum(0, keepdims=True)
        dp = dot(vv, do2t)
        ds = (w * (dp - delta) * scaling).astype(jnp.bfloat16)
        ds_all[:, span] = ds
        dqt = dot(kt, ds).astype(jnp.bfloat16)
        for j in range(2):
            h = 2 * pair + j
            out_ref[:, h * HD : (h + 1) * HD] = ot[:, j * rows : (j + 1) * rows].T
            dq_ref[:, h * HD : (h + 1) * HD] = dqt[:, j * rows : (j + 1) * rows].T
    dk = dot(ds_all[...], q_all[...]).astype(jnp.bfloat16)
    dv = dot(wl_all[...], do_all[...]).astype(jnp.bfloat16)
    dok_ref[...] = dk[prefix:, :]
    dov_ref[...] = dv[prefix:, :]
    for i in range(entries):
        start = pl.multiple_of(list_ref[me, i] * block_rows, block_rows)
        dpkv_ref[pl.ds(start, block_rows), key_cols] = dk[i * block_rows : (i + 1) * block_rows, :]
        dpkv_ref[pl.ds(start, block_rows), value_cols] = dv[i * block_rows : (i + 1) * block_rows, :]


def attention(block_list, block_count, length, queries, grads, prompt, own_keys, own_values, block_rows):
    rows, width = queries.shape
    slot_rows = prompt.shape[0]
    total = block_list.shape[1] * block_rows + rows
    wide = pl.BlockSpec((rows, GROUP * HD), lambda g, *_: (0, g))
    own = pl.BlockSpec((rows, HD), lambda g, *_: (0, g))
    shared = pl.BlockSpec(memory_space=pltpu.VMEM)
    low = jnp.bfloat16
    return pl.pallas_call(
        functools.partial(attention_kernel, block_rows),
        grid_spec=pltpu.PrefetchScalarGridSpec(
            num_scalar_prefetch=3,
            grid=(KVH,),
            in_specs=[wide, wide, shared, own, own],
            out_specs=[wide, wide, own, own, shared],
            scratch_shapes=[
                pltpu.VMEM((total, HD), low),
                pltpu.VMEM((total, HD), low),
                pltpu.VMEM((total, 2 * rows), jnp.float32),
                pltpu.VMEM((total, GROUP * rows), low),
                pltpu.VMEM((total, GROUP * rows), low),
                pltpu.VMEM((GROUP * rows, HD), low),
                pltpu.VMEM((GROUP * rows, HD), low),
            ],
        ),
        out_shape=[
            jax.ShapeDtypeStruct((rows, width), low),
            jax.ShapeDtypeStruct((rows, width), low),
            jax.ShapeDtypeStruct((rows, KVH * HD), low),
            jax.ShapeDtypeStruct((rows, KVH * HD), low),
            jax.ShapeDtypeStruct((slot_rows, 2 * KVH * HD), low),
        ],
        compiler_params=pltpu.CompilerParams(vmem_limit_bytes=(40 << 20) - 4 * prompt.size),
        name="attention",
    )(block_list, block_count, length, queries, grads, prompt, own_keys, own_values)


MESH = pl.DeviceIdType.MESH


def plane(n):
    me = lax.axis_index("seq")
    z, y, c = me // 4, lax.rem(me // 2, 2), lax.rem(me, 2)

    def index(dz, y, c):
        return lax.rem(z + dz + n // 4, n // 4) * 4 + y * 2 + c

    return me, y, c, index


def greet(peers):
    barrier = pltpu.get_barrier_semaphore()
    for peer in peers:
        pl.semaphore_signal(barrier, inc=1, device_id={"seq": peer}, device_id_type=MESH)
    pl.semaphore_wait(barrier, len(peers))


def gather_kernel(n, parts, k_ref, v_ref, all_ref, own_sem, zs, zr, ys, yr, cs, cr):
    me, y, c, index = plane(n)
    nz = n // 4
    size, width = k_ref.shape
    step = size // parts

    def at(source, part):
        return all_ref.at[pl.ds(pl.multiple_of(source * size + part * step, step), step), :]

    mine = pl.ds(pl.multiple_of(me * size, size), size)
    loads = [
        pltpu.make_async_copy(k_ref, all_ref.at[mine, :width], own_sem.at[0]),
        pltpu.make_async_copy(v_ref, all_ref.at[mine, width:], own_sem.at[1]),
    ]
    for one in loads:
        one.start()
    across, partner = index(0, 1 - y, c), index(0, y, 1 - c)
    greet([index(dz, y, c) for dz in range(1, nz)] + [across, partner])
    for one in loads:
        one.wait()

    def copy(source, part, send, recv, slot, peer):
        return pltpu.make_async_remote_copy(
            src_ref=at(source, part),
            dst_ref=at(source, part),
            send_sem=send.at[slot * parts + part],
            recv_sem=recv.at[slot * parts + part],
            device_id={"seq": peer},
            device_id_type=MESH,
        )

    started = []

    def start(*args):
        started.append(copy(*args))
        started[-1].start()

    for part in range(parts):
        for dz in range(1, nz):
            start(me, part, zs, zr, dz, index(dz, y, c))
        start(me, part, ys, yr, 0, across)
        start(me, part, cs, cr, 0, partner)

    def over(dz, part):
        source = index(-dz, 1 - y, c)
        copy(source, part, ys, yr, dz, across).wait_recv()
        start(source, part, cs, cr, nz + dz, partner)

    pending = []
    for part in range(parts):
        for dz in range(1, nz):
            source = index(-dz, y, c)
            copy(source, part, zs, zr, dz, across).wait_recv()
            start(source, part, ys, yr, dz, across)
            start(source, part, cs, cr, dz, partner)
        for one in pending:
            over(*one)
        pending = [(dz, part) for dz in range(1, nz)] + [(0, part)]
    for one in pending:
        over(*one)
    for part in range(parts):
        for dz in range(nz):
            copy(index(-dz, y, 1 - c), part, cs, cr, dz, partner).wait_recv()
            copy(index(-dz, 1 - y, 1 - c), part, cs, cr, nz + dz, partner).wait_recv()
    for one in started:
        one.wait_send()


def gather(keys, values, n):
    rows, width = keys.shape
    nz = n // 4
    vmem = pl.BlockSpec(memory_space=pltpu.VMEM)
    dma = pltpu.SemaphoreType.DMA
    parts = math.gcd(rows // 16, PARTS)
    some, more = dma((parts * nz,)), dma((parts * 2 * nz,))
    return pl.pallas_call(
        functools.partial(gather_kernel, n, parts),
        in_specs=[pl.BlockSpec(memory_space=pl.ANY)] * 2,
        out_specs=vmem,
        out_shape=jax.ShapeDtypeStruct((n * rows, 2 * width), keys.dtype),
        scratch_shapes=[dma((2,)), some, some, some, some, more, more],
        compiler_params=pltpu.CompilerParams(
            collective_id=0, has_side_effects=True, vmem_limit_bytes=(50 << 20) - 4 * n * rows * width
        ),
        name="gather",
    )(keys, values)


def scatter_kernel(n, parts, t_ref, pk_ref, pv_ref, crecv, yrecv, zrecv, ysend, zsend, cs, cr, ys, yr, zs, zr):
    me, y, c, index = plane(n)
    nz = n // 4
    size, width = pk_ref.shape
    step = size // parts
    across, partner = index(0, 1 - y, c), index(0, y, 1 - c)

    def at(owner, part):
        return t_ref.at[pl.ds(pl.multiple_of(owner * size + part * step, step), step), :]

    def copy(source, target, send, recv, slot, peer):
        return pltpu.make_async_remote_copy(
            src_ref=source,
            dst_ref=target.at[slot],
            send_sem=send.at[slot],
            recv_sem=recv.at[slot],
            device_id={"seq": peer},
            device_id_type=MESH,
        )

    greet([index(dz, y, c) for dz in range(1, nz)] + [across, partner])
    distances = sorted(range(1, nz), key=lambda dz: abs(2 * dz - nz)) + [0]
    order = [(dz, part) for dz in distances for part in range(parts)]
    inside, over, along = {}, {}, {}
    for far in (1, 0):
        for dz, part in order:
            slot = (2 * dz + far) * parts + part
            owner = index(dz, 1 - y if far else y, 1 - c)
            inside[slot] = copy(at(owner, part), crecv, cs, cr, slot, partner)
            inside[slot].start()
    for dz, part in order:
        slot, out = (2 * dz + 1) * parts + part, dz * parts + part
        inside[slot].wait_recv()
        mine = at(index(dz, 1 - y, c), part)[...].astype(jnp.float32)
        ysend[out] = (mine + crecv[slot].astype(jnp.float32)).astype(ysend.dtype)
        over[out] = copy(ysend.at[out], yrecv, ys, yr, out, across)
        over[out].start()
    totals = {}
    for dz, part in order:
        slot, out = 2 * dz * parts + part, dz * parts + part
        inside[slot].wait_recv()
        mine = at(index(dz, y, c), part)[...].astype(jnp.float32) + crecv[slot].astype(jnp.float32)
        over[out].wait_recv()
        mine = mine + yrecv[out].astype(jnp.float32)
        if dz:
            zsend[out] = mine.astype(zsend.dtype)
            along[out] = copy(zsend.at[out], zrecv, zs, zr, out, index(dz, y, c))
            along[out].start()
        else:
            totals[part] = mine
    for part in range(parts):
        total = totals[part]
        for dz in distances[:-1]:
            along[dz * parts + part].wait_recv()
            total = total + zrecv[dz * parts + part].astype(jnp.float32)
        total = total.astype(pk_ref.dtype)
        pk_ref[part * step : (part + 1) * step, :] = total[:, :width]
        pv_ref[part * step : (part + 1) * step, :] = total[:, width:]
    for one in [*inside.values(), *over.values(), *along.values()]:
        one.wait_send()


def scatter(terms, n):
    rows, width = terms.shape[0] // n, terms.shape[1]
    nz = n // 4
    vmem = pl.BlockSpec(memory_space=pltpu.VMEM)
    dma = pltpu.SemaphoreType.DMA
    parts = math.gcd(rows // 16, 2)
    block = (nz * parts, rows // parts, width)
    low = terms.dtype
    return pl.pallas_call(
        functools.partial(scatter_kernel, n, parts),
        in_specs=[vmem],
        out_specs=[vmem, vmem],
        out_shape=[jax.ShapeDtypeStruct((rows, width // 2), low)] * 2,
        scratch_shapes=[
            pltpu.VMEM((2 * nz * parts, rows // parts, width), low),
            pltpu.VMEM(block, low),
            pltpu.VMEM(block, low),
            pltpu.VMEM(block, low),
            pltpu.VMEM(block, low),
            dma((2 * nz * parts,)),
            dma((2 * nz * parts,)),
            dma((nz * parts,)),
            dma((nz * parts,)),
            dma((nz * parts,)),
            dma((nz * parts,)),
        ],
        compiler_params=pltpu.CompilerParams(
            collective_id=1, has_side_effects=True, vmem_limit_bytes=40 << 20
        ),
        name="scatter",
    )(terms)


def per_device(
    queries,
    response_keys,
    response_values,
    output_grad,
    prompt_keys,
    prompt_values,
    block_list,
    block_count,
    response_length,
):
    block_rows = prompt_keys.shape[0] // 2
    n = lax.axis_size("seq")
    prompt = gather(prompt_keys, prompt_values, n)
    out, dq, dok, dov, terms = attention(
        block_list,
        block_count,
        response_length,
        queries,
        output_grad,
        prompt,
        response_keys,
        response_values,
        block_rows,
    )
    dpk, dpv = scatter(terms, n)
    return out, dq, dok, dov, dpk, dpv


def solution(mesh):
    both = P(("group", "seq"), None)
    return jax.shard_map(
        per_device,
        mesh=mesh,
        in_specs=(both, both, both, both, both, both, P("group", None), P("group"), P(("group", "seq"))),
        out_specs=(both,) * 6,
        check_vma=False,
    )
```

```python
import functools
import math

import jax
import jax.numpy as jnp
from jax import lax
from jax.experimental import pallas as pl
from jax.experimental.pallas import tpu as pltpu
from jax.sharding import PartitionSpec as P

HD = 128
QH = 32
KVH = 4
GROUP = QH // KVH

PARTS = 2
MASKED = -1e30


def dot(a, b, ca=1, cb=0):
    return lax.dot_general(
        a, b, (((ca,), (cb,)), ((), ())), preferred_element_type=jnp.float32
    )


def attention_kernel(
    block_rows,
    list_ref,
    count_ref,
    length_ref,
    q_ref,
    do_ref,
    pkv_ref,
    ok_ref,
    ov_ref,
    out_ref,
    dq_ref,
    dok_ref,
    dov_ref,
    dpkv_ref,
    k_all,
    v_all,
    bias,
    ds_all,
    wl_all,
    q_all,
    do_all,
):
    rows = q_ref.shape[0]
    entries = list_ref.shape[1]
    me = lax.axis_index("seq")
    g = pl.program_id(0)
    key_cols = pl.ds(pl.multiple_of(g * HD, HD), HD)
    value_cols = pl.ds(pl.multiple_of((KVH + g) * HD, HD), HD)
    prefix = entries * block_rows
    keys = prefix + rows
    scaling = 1.0 / math.sqrt(HD)
    count, length = count_ref[me], length_ref[0]

    @pl.when(g == 0)
    def _():
        key_row = lax.broadcasted_iota(jnp.int32, (prefix, 2 * rows), 0)
        bias[:prefix, :] = jnp.where(key_row < count * block_rows, 0.0, MASKED)
        own = lax.broadcasted_iota(jnp.int32, (rows, rows), 0)
        tok = lax.broadcasted_iota(jnp.int32, (rows, rows), 1)
        own_bias = jnp.where((own <= tok) & (own < length), 0.0, MASKED)
        bias[prefix:, :rows] = own_bias
        bias[prefix:, rows:] = own_bias
        dpkv_ref[...] = jnp.zeros_like(dpkv_ref)

    for i in range(entries):
        start = pl.multiple_of(list_ref[me, i] * block_rows, block_rows)
        k_all[i * block_rows : (i + 1) * block_rows, :] = pkv_ref[pl.ds(start, block_rows), key_cols]
        v_all[i * block_rows : (i + 1) * block_rows, :] = pkv_ref[pl.ds(start, block_rows), value_cols]
    k_all[prefix:, :] = ok_ref[...]
    v_all[prefix:, :] = ov_ref[...]
    kk, vv = k_all[...], v_all[...]
    kt, vt = kk.T, vv.T
    live = (lax.broadcasted_iota(jnp.int32, (rows, HD), 0) < length).astype(jnp.float32)
    live = live.astype(jnp.bfloat16)
    for h in range(GROUP):
        q_all[h * rows : (h + 1) * rows, :] = q_ref[:, h * HD : (h + 1) * HD]
        do_all[h * rows : (h + 1) * rows, :] = do_ref[:, h * HD : (h + 1) * HD] * live
    for pair in range(GROUP // 2):
        span = slice(pair * 2 * rows, (pair + 1) * 2 * rows)
        q2, do2 = q_all[span, :], do_all[span, :]
        do2t = do2.T
        s = dot(kk, q2, 1, 1) * (scaling * math.log2(math.e)) + bias[...]
        e = jnp.exp2(s - s.max(0, keepdims=True))
        w = e * (1.0 / e.sum(0, keepdims=True))
        wl = w.astype(jnp.bfloat16)
        wl_all[:, span] = wl
        ot = dot(vt, wl).astype(jnp.bfloat16)
        delta = (do2t.astype(jnp.float32) * ot.astype(jnp.float32)).sum(0, keepdims=True)
        dp = dot(vv, do2t)
        ds = (w * (dp - delta)).astype(jnp.bfloat16)
        ds_all[:, span] = ds
        dqt = (dot(kt, ds) * scaling).astype(jnp.bfloat16)
        for j in range(2):
            h = 2 * pair + j
            out_ref[:, h * HD : (h + 1) * HD] = ot[:, j * rows : (j + 1) * rows].T
            dq_ref[:, h * HD : (h + 1) * HD] = dqt[:, j * rows : (j + 1) * rows].T
    dk = (dot(ds_all[...], q_all[...]) * scaling).astype(jnp.bfloat16)
    dv = dot(wl_all[...], do_all[...]).astype(jnp.bfloat16)
    dok_ref[...] = dk[prefix:, :]
    dov_ref[...] = dv[prefix:, :]
    for i in range(entries):
        start = pl.multiple_of(list_ref[me, i] * block_rows, block_rows)
        dpkv_ref[pl.ds(start, block_rows), key_cols] = dk[i * block_rows : (i + 1) * block_rows, :]
        dpkv_ref[pl.ds(start, block_rows), value_cols] = dv[i * block_rows : (i + 1) * block_rows, :]


def attention(block_list, block_count, length, queries, grads, prompt, own_keys, own_values, block_rows):
    rows, width = queries.shape
    slot_rows = prompt.shape[0]
    total = block_list.shape[1] * block_rows + rows
    wide = pl.BlockSpec((rows, GROUP * HD), lambda g, *_: (0, g))
    own = pl.BlockSpec((rows, HD), lambda g, *_: (0, g))
    shared = pl.BlockSpec(memory_space=pltpu.VMEM)
    low = jnp.bfloat16
    return pl.pallas_call(
        functools.partial(attention_kernel, block_rows),
        grid_spec=pltpu.PrefetchScalarGridSpec(
            num_scalar_prefetch=3,
            grid=(KVH,),
            in_specs=[wide, wide, shared, own, own],
            out_specs=[wide, wide, own, own, shared],
            scratch_shapes=[
                pltpu.VMEM((total, HD), low),
                pltpu.VMEM((total, HD), low),
                pltpu.VMEM((total, 2 * rows), jnp.float32),
                pltpu.VMEM((total, GROUP * rows), low),
                pltpu.VMEM((total, GROUP * rows), low),
                pltpu.VMEM((GROUP * rows, HD), low),
                pltpu.VMEM((GROUP * rows, HD), low),
            ],
        ),
        out_shape=[
            jax.ShapeDtypeStruct((rows, width), low),
            jax.ShapeDtypeStruct((rows, width), low),
            jax.ShapeDtypeStruct((rows, KVH * HD), low),
            jax.ShapeDtypeStruct((rows, KVH * HD), low),
            jax.ShapeDtypeStruct((slot_rows, 2 * KVH * HD), low),
        ],
        compiler_params=pltpu.CompilerParams(vmem_limit_bytes=(40 << 20) - 4 * prompt.size),
        name="attention",
    )(block_list, block_count, length, queries, grads, prompt, own_keys, own_values)


MESH = pl.DeviceIdType.MESH


def plane(n):
    me = lax.axis_index("seq")
    z, y, c = me // 4, lax.rem(me // 2, 2), lax.rem(me, 2)

    def index(dz, y, c):
        return lax.rem(z + dz + n // 4, n // 4) * 4 + y * 2 + c

    return me, y, c, index


def greet(peers):
    barrier = pltpu.get_barrier_semaphore()
    for peer in peers:
        pl.semaphore_signal(barrier, inc=1, device_id={"seq": peer}, device_id_type=MESH)
    pl.semaphore_wait(barrier, len(peers))


def gather_kernel(n, parts, k_ref, v_ref, all_ref, own_sem, zs, zr, ys, yr, cs, cr):
    me, y, c, index = plane(n)
    nz = n // 4
    size, width = k_ref.shape
    step = size // parts

    def at(source, part):
        return all_ref.at[pl.ds(pl.multiple_of(source * size + part * step, step), step), :]

    mine = pl.ds(pl.multiple_of(me * size, size), size)
    loads = [
        pltpu.make_async_copy(k_ref, all_ref.at[mine, :width], own_sem.at[0]),
        pltpu.make_async_copy(v_ref, all_ref.at[mine, width:], own_sem.at[1]),
    ]
    for one in loads:
        one.start()
    across, partner = index(0, 1 - y, c), index(0, y, 1 - c)
    greet([index(dz, y, c) for dz in range(1, nz)] + [across, partner])
    for one in loads:
        one.wait()

    def copy(source, part, send, recv, slot, peer):
        return pltpu.make_async_remote_copy(
            src_ref=at(source, part),
            dst_ref=at(source, part),
            send_sem=send.at[slot * parts + part],
            recv_sem=recv.at[slot * parts + part],
            device_id={"seq": peer},
            device_id_type=MESH,
        )

    started = []

    def start(*args):
        started.append(copy(*args))
        started[-1].start()

    for part in range(parts):
        for dz in range(1, nz):
            start(me, part, zs, zr, dz, index(dz, y, c))
        start(me, part, ys, yr, 0, across)
        start(me, part, cs, cr, 0, partner)

    def over(dz, part):
        source = index(-dz, 1 - y, c)
        copy(source, part, ys, yr, dz, across).wait_recv()
        start(source, part, cs, cr, nz + dz, partner)

    pending = []
    for part in range(parts):
        for dz in range(1, nz):
            source = index(-dz, y, c)
            copy(source, part, zs, zr, dz, across).wait_recv()
            start(source, part, ys, yr, dz, across)
            start(source, part, cs, cr, dz, partner)
        for one in pending:
            over(*one)
        pending = [(dz, part) for dz in range(1, nz)] + [(0, part)]
    for one in pending:
        over(*one)
    for part in range(parts):
        for dz in range(nz):
            copy(index(-dz, y, 1 - c), part, cs, cr, dz, partner).wait_recv()
            copy(index(-dz, 1 - y, 1 - c), part, cs, cr, nz + dz, partner).wait_recv()
    for one in started:
        one.wait_send()


def gather(keys, values, n):
    rows, width = keys.shape
    nz = n // 4
    vmem = pl.BlockSpec(memory_space=pltpu.VMEM)
    dma = pltpu.SemaphoreType.DMA
    parts = math.gcd(rows // 16, PARTS)
    some, more = dma((parts * nz,)), dma((parts * 2 * nz,))
    return pl.pallas_call(
        functools.partial(gather_kernel, n, parts),
        in_specs=[pl.BlockSpec(memory_space=pl.ANY)] * 2,
        out_specs=vmem,
        out_shape=jax.ShapeDtypeStruct((n * rows, 2 * width), keys.dtype),
        scratch_shapes=[dma((2,)), some, some, some, some, more, more],
        compiler_params=pltpu.CompilerParams(
            collective_id=0, has_side_effects=True, vmem_limit_bytes=(50 << 20) - 4 * n * rows * width
        ),
        name="gather",
    )(keys, values)


def scatter_kernel(n, parts, t_ref, pk_ref, pv_ref, crecv, yrecv, zrecv, ysend, zsend, cs, cr, ys, yr, zs, zr):
    me, y, c, index = plane(n)
    nz = n // 4
    size, width = pk_ref.shape
    step = size // parts
    across, partner = index(0, 1 - y, c), index(0, y, 1 - c)

    def at(owner, part):
        return t_ref.at[pl.ds(pl.multiple_of(owner * size + part * step, step), step), :]

    def copy(source, target, send, recv, slot, peer):
        return pltpu.make_async_remote_copy(
            src_ref=source,
            dst_ref=target.at[slot],
            send_sem=send.at[slot],
            recv_sem=recv.at[slot],
            device_id={"seq": peer},
            device_id_type=MESH,
        )

    greet([index(dz, y, c) for dz in range(1, nz)] + [across, partner])
    distances = sorted(range(1, nz), key=lambda dz: abs(2 * dz - nz)) + [0]
    order = [(dz, part) for dz in distances for part in range(parts)]
    inside, over, along = {}, {}, {}
    for far in (1, 0):
        for dz, part in order:
            slot = (2 * dz + far) * parts + part
            owner = index(dz, 1 - y if far else y, 1 - c)
            inside[slot] = copy(at(owner, part), crecv, cs, cr, slot, partner)
            inside[slot].start()
    for dz, part in order:
        slot, out = (2 * dz + 1) * parts + part, dz * parts + part
        inside[slot].wait_recv()
        mine = at(index(dz, 1 - y, c), part)[...].astype(jnp.float32)
        ysend[out] = (mine + crecv[slot].astype(jnp.float32)).astype(ysend.dtype)
        over[out] = copy(ysend.at[out], yrecv, ys, yr, out, across)
        over[out].start()
    totals = {}
    for dz, part in order:
        slot, out = 2 * dz * parts + part, dz * parts + part
        inside[slot].wait_recv()
        mine = at(index(dz, y, c), part)[...].astype(jnp.float32) + crecv[slot].astype(jnp.float32)
        over[out].wait_recv()
        mine = mine + yrecv[out].astype(jnp.float32)
        if dz:
            zsend[out] = mine.astype(zsend.dtype)
            along[out] = copy(zsend.at[out], zrecv, zs, zr, out, index(dz, y, c))
            along[out].start()
        else:
            totals[part] = mine
    for part in range(parts):
        total = totals[part]
        for dz in distances[:-1]:
            along[dz * parts + part].wait_recv()
            total = total + zrecv[dz * parts + part].astype(jnp.float32)
        total = total.astype(pk_ref.dtype)
        pk_ref[part * step : (part + 1) * step, :] = total[:, :width]
        pv_ref[part * step : (part + 1) * step, :] = total[:, width:]
    for one in [*inside.values(), *over.values(), *along.values()]:
        one.wait_send()


def scatter(terms, n):
    rows, width = terms.shape[0] // n, terms.shape[1]
    nz = n // 4
    vmem = pl.BlockSpec(memory_space=pltpu.VMEM)
    dma = pltpu.SemaphoreType.DMA
    parts = math.gcd(rows // 16, 2)
    block = (nz * parts, rows // parts, width)
    low = terms.dtype
    return pl.pallas_call(
        functools.partial(scatter_kernel, n, parts),
        in_specs=[vmem],
        out_specs=[vmem, vmem],
        out_shape=[jax.ShapeDtypeStruct((rows, width // 2), low)] * 2,
        scratch_shapes=[
            pltpu.VMEM((2 * nz * parts, rows // parts, width), low),
            pltpu.VMEM(block, low),
            pltpu.VMEM(block, low),
            pltpu.VMEM(block, low),
            pltpu.VMEM(block, low),
            dma((2 * nz * parts,)),
            dma((2 * nz * parts,)),
            dma((nz * parts,)),
            dma((nz * parts,)),
            dma((nz * parts,)),
            dma((nz * parts,)),
        ],
        compiler_params=pltpu.CompilerParams(
            collective_id=1, has_side_effects=True, vmem_limit_bytes=40 << 20
        ),
        name="scatter",
    )(terms)


def per_device(
    queries,
    response_keys,
    response_values,
    output_grad,
    prompt_keys,
    prompt_values,
    block_list,
    block_count,
    response_length,
):
    block_rows = prompt_keys.shape[0] // 2
    n = lax.axis_size("seq")
    prompt = gather(prompt_keys, prompt_values, n)
    out, dq, dok, dov, terms = attention(
        block_list,
        block_count,
        response_length,
        queries,
        output_grad,
        prompt,
        response_keys,
        response_values,
        block_rows,
    )
    dpk, dpv = scatter(terms, n)
    return out, dq, dok, dov, dpk, dpv


def solution(mesh):
    both = P(("group", "seq"), None)
    return jax.shard_map(
        per_device,
        mesh=mesh,
        in_specs=(both, both, both, both, both, both, P("group", None), P("group"), P(("group", "seq"))),
        out_specs=(both,) * 6,
        check_vma=False,
    )
```
